32 devices in a mesh: bx: 8 (over z, x), by: 4 (over y, core).
Axes of the slice: x: 2, y: 2, z: 4, core: 2. Of those that a mesh axis runs over, the one named last changes fastest.
Arguments:
- features: bfloat16 [8, 4, 1024, 128], P('bx', 'by'), may hold values from -13 to 13
- live_count: int32 [8, 4], P('bx', 'by'), may hold values from 128 to 1024, as said below
- neighbour_map: int32 [8, 4, 27, 1024], P('bx', 'by'), may hold values from 0 to 2175, as said below
- send_rows: int32 [8, 4, 8, 128], P('bx', 'by'), may hold values from 0 to 1023, as said below
- weight: bfloat16 [3456, 128], replicated, may hold values from -0.109375 to 0.109375
- gain: float32 [128], replicated, may hold values from 0.5 to 1.5
- shift: float32 [128], replicated, may hold values from -3 to 3
- cotangent: bfloat16 [8, 4, 1024, 128], P('bx', 'by'), may hold values from -13 to 13
Outputs:
- activated: bfloat16 [8, 4, 1024, 128], P('bx', 'by')
- grad_features: bfloat16 [8, 4, 1024, 128], P('bx', 'by')
- grad_weight: float32 [27, 128, 128], P(None, 'bx', 'by')
The draws below stay inside these ranges and needn't reach their ends.
Inputs may be any that keep to these rules, and one draw needn't show every extreme that they name: Rows 0 to live_count - 1 of a brick are live, the rest padding; in every draw some brick is full. `send_rows`: every entry is below its brick's live count; the eight blocks follow the directions (dx, dy) in row-major order with the brick's own position left out. `neighbour_map`: entries index the brick's extended table; offset 13 of a live row names that row itself; every entry of a padding row is 1536. With B = min(1024, 512) and q = r // B for a live row r, an entry below 1024 lies in rows q B to q B + B - 1, and an entry 1024 + b * 128 + h of incoming block b other than 4 has h in q * 128 B / 1024 to (q + 1) * 128 B / 1024 - 1.
All inputs are finite; a program needn't handle non-finite values.
Results may differ from the reference program's by a relative error of at most 0.029.
The reference program's roundings to bfloat16 on the way (of `outgoing`, `incoming`, `extended`, `conv_out`, `conv_grad`, `halo_grad` and `returned`) count: a program that leaves them out, or rounds other values in their place, can miss the bound.
Values may be sent and summed in bfloat16 or wider, within the bound.
A program may use at most 64 MiB of HBM per device.

```python
import jax
import jax.numpy as jnp
from jax import lax

C = 128
OFFSETS = 27
ROWS = 1024
HALO = 128
BRICKS_X = 8
BRICKS_Y = 4


def brick_counts(key):
    bricks = BRICKS_X * BRICKS_Y
    levels = jax.random.randint(jax.random.fold_in(key, 11), (bricks,), 0, 1024)
    spread = ROWS - ROWS // 8
    counts = ROWS // 8 + spread * (levels * levels // 1024) // 1023
    fullest = jax.random.randint(jax.random.fold_in(key, 12), (), 0, bricks)
    counts = jnp.where(jnp.arange(bricks) == fullest, ROWS, counts)
    return counts.reshape(BRICKS_X, BRICKS_Y).astype(jnp.int32)


def draw_live_count(key, part):
    return brick_counts(key)


def draw_send_rows(key, part):
    counts = brick_counts(key)[:, :, None, None]
    return jax.random.randint(jax.random.fold_in(key, 21), (BRICKS_X, BRICKS_Y, 8, HALO), 0, counts).astype(jnp.int32)


def draw_neighbour_map(key, part):
    counts = brick_counts(key)[:, :, None, None]
    shape = (BRICKS_X, BRICKS_Y, OFFSETS, ROWS)
    block_rows = min(ROWS, 512)
    halo_window = HALO // (ROWS // block_rows)
    row_ids = jnp.arange(ROWS, dtype=jnp.int32)[None, None, None, :]
    block_index = row_ids // block_rows
    start = block_index * block_rows
    room = jnp.maximum(jnp.minimum(block_rows, counts - start), 1)
    kinds = jax.random.randint(jax.random.fold_in(key, 31), shape, 0, 8)
    local = start + jax.random.randint(jax.random.fold_in(key, 32), shape, 0, room)
    slot = jax.random.randint(jax.random.fold_in(key, 33), shape, 0, 8)
    target = slot + (slot >= 4).astype(jnp.int32)
    remote = ROWS + target * HALO + block_index * halo_window + jax.random.randint(jax.random.fold_in(key, 34), shape, 0, halo_window)
    absent = ROWS + 4 * HALO
    chosen = jnp.where(kinds < 3, absent, jnp.where(kinds < 6, local, remote))
    offset_ids = jnp.arange(OFFSETS, dtype=jnp.int32)[None, None, :, None]
    chosen = jnp.where(offset_ids == 13, row_ids, chosen)
    chosen = jnp.where(row_ids < counts, chosen, absent)
    return chosen.astype(jnp.int32)


def rising_field(key):
    shape = (BRICKS_X, BRICKS_Y, ROWS, C)
    position = (jnp.arange(BRICKS_X)[:, None] * BRICKS_Y + jnp.arange(BRICKS_Y)[None, :]).astype(jnp.float32)
    rise = 1.0 + 2.0 * position / max(BRICKS_X * BRICKS_Y - 1, 1)
    base = jax.random.truncated_normal(jax.random.fold_in(key, 41), -4.0, 4.0, shape, jnp.float32)
    offsets = jax.random.uniform(jax.random.fold_in(key, 42), (C,), jnp.float32, -1.0, 1.0)
    return (base * rise[:, :, None, None] + offsets).astype(jnp.bfloat16)


def draw_features(key, part):
    return rising_field(jax.random.fold_in(key, 51))


def draw_cotangent(key, part):
    return rising_field(jax.random.fold_in(key, 52))


def normal_values(key, dims, scale, bound, kind=jnp.bfloat16):
    return jnp.clip(scale * jax.random.normal(key, dims, jnp.float32), -bound, bound).astype(kind)


def setup_inputs(seed: int = 0) -> dict:
    splits = jax.random.split(jax.random.key(seed), 9)
    features = draw_features(jax.random.fold_in(splits[8], 71), 0)
    live_count = draw_live_count(jax.random.fold_in(splits[8], 71), 0)
    neighbour_map = draw_neighbour_map(jax.random.fold_in(splits[8], 71), 0)
    send_rows = draw_send_rows(jax.random.fold_in(splits[8], 71), 0)
    weight = normal_values(splits[4], (OFFSETS * C, C), (OFFSETS * C) ** -0.5, 0.109375)
    gain = jnp.clip(1.0 + 0.1 * jax.random.normal(splits[5], (C,), jnp.float32), 0.5, 1.5)
    shift = normal_values(splits[6], (C,), 0.5, 3.0, jnp.float32)
    cotangent = draw_cotangent(jax.random.fold_in(splits[8], 71), 0)
    return {"features": features, "live_count": live_count, "neighbour_map": neighbour_map, "send_rows": send_rows, "weight": weight, "gain": gain, "shift": shift, "cotangent": cotangent}


def incoming_blocks(blocks):
    padded = jnp.pad(blocks, ((1, 1), (1, 1), (0, 0), (0, 0), (0, 0)))
    parts = []
    for place in range(9):
        first = place // 3
        second = place % 3
        parts.append(padded[first:first + BRICKS_X, second:second + BRICKS_Y, 8 - place])
    return jnp.stack(parts, axis=2)

def reference(features, live_count, neighbour_map, send_rows, weight, gain, shift, cotangent):
    bricks = BRICKS_X * BRICKS_Y
    picked = jax.vmap(jax.vmap(lambda rows, index: rows[index.reshape(-1)]))(features, send_rows)
    picked = picked.reshape(BRICKS_X, BRICKS_Y, 8, HALO, C)
    empty = jnp.zeros((BRICKS_X, BRICKS_Y, 1, HALO, C), jnp.bfloat16)
    outgoing = jnp.concatenate([picked[:, :, :4], empty, picked[:, :, 4:]], axis=2)
    incoming = incoming_blocks(outgoing).reshape(BRICKS_X, BRICKS_Y, 9 * HALO, C)
    extended = jnp.concatenate([features, incoming], axis=2).reshape(bricks, ROWS + 9 * HALO, C)
    maps = neighbour_map.reshape(bricks, OFFSETS, ROWS)

    def forward_one(pair):
        table, indices = pair
        columns = table[indices.T.reshape(-1)].reshape(ROWS, OFFSETS * C)
        return jnp.dot(columns, weight, preferred_element_type=jnp.float32).astype(jnp.bfloat16)
    conv_out = lax.map(forward_one, (extended, maps))
    conv_float = conv_out.astype(jnp.float32)
    row_ids = jnp.arange(ROWS, dtype=jnp.int32)
    live = (row_ids[None, :] < live_count.reshape(bricks, 1)).astype(jnp.float32)[:, :, None]
    total = jnp.sum(live_count.astype(jnp.float32))
    center = lax.optimization_barrier(jnp.sum(conv_float * live, axis=(0, 1))) / total
    deviation = (conv_float - center) * live
    variance = lax.optimization_barrier(jnp.sum(deviation * deviation, axis=(0, 1))) / total
    inverse_std = lax.rsqrt(variance + 1e-05)
    normalized = (conv_float - center) * inverse_std
    before = gain * normalized + shift
    activated = (jnp.maximum(before, 0.0) * live).astype(jnp.bfloat16)
    upstream = cotangent.reshape(bricks, ROWS, C).astype(jnp.float32) * (before > 0.0) * live
    sum_up = lax.optimization_barrier(jnp.sum(upstream, axis=(0, 1)))
    sum_cross = lax.optimization_barrier(jnp.sum(upstream * normalized, axis=(0, 1)))
    conv_grad = (gain * inverse_std * (upstream - live * (sum_up + normalized * sum_cross) / total)).astype(jnp.bfloat16)

    def backward_one(weight_acc, triple):
        table, indices, grad_rows = triple
        columns = table[indices.T.reshape(-1)].reshape(ROWS, OFFSETS * C)
        weight_acc = weight_acc + jnp.dot(columns.T, grad_rows, preferred_element_type=jnp.float32)
        column_grad = jnp.dot(grad_rows, weight.T, preferred_element_type=jnp.float32)
        table_grad = jnp.zeros((ROWS + 9 * HALO, C), jnp.float32).at[indices.T.reshape(-1)].add(column_grad.reshape(-1, C))
        return (weight_acc, table_grad)
    weight_sum, table_grads = lax.scan(backward_one, jnp.zeros((OFFSETS * C, C), jnp.float32), (extended, maps, conv_grad))
    grad_weight = (weight_sum / jnp.sqrt(total)).reshape(OFFSETS, C, C)
    halo_grad = table_grads[:, ROWS:].astype(jnp.bfloat16).reshape(BRICKS_X, BRICKS_Y, 9, HALO, C)
    returned = incoming_blocks(halo_grad)
    slots = jnp.concatenate([returned[:, :, :4], returned[:, :, 5:]], axis=2).reshape(BRICKS_X, BRICKS_Y, 8 * HALO, C).astype(jnp.float32)
    own_grad = table_grads[:, :ROWS].reshape(BRICKS_X, BRICKS_Y, ROWS, C)
    own_grad = jax.vmap(jax.vmap(lambda grads, index, added: grads.at[index.reshape(-1)].add(added)))(own_grad, send_rows, slots)
    return (activated.reshape(BRICKS_X, BRICKS_Y, ROWS, C), own_grad.astype(jnp.bfloat16), grad_weight)
```

```python
import functools

import jax
import jax.numpy as jnp
from jax import lax
from jax.experimental import pallas as pl
from jax.experimental.pallas import tpu as pltpu
from jax.sharding import PartitionSpec as P

epsilon = 1e-05
OFFSETS = 27
GROUP = 3
MESH = pl.DeviceIdType.MESH
f32 = jnp.float32
bf16 = jnp.bfloat16


def one_hot(mask):
    return jnp.where(mask, 1.0, 0.0).astype(bf16)


def lanes_from_row(row):
    return jnp.broadcast_to(row, (128, row.shape[1])).T


def row_selector(row, width):
    wide = lanes_from_row(row)
    lane = lax.broadcasted_iota(jnp.int32, wide.shape, 1)
    return jnp.concatenate([one_hot(wide == lane + j) for j in range(0, width, 128)], axis=1)


def kernel(
    nx, ny, live_ref, feat, nmap, send, weight, gain, shift, cot,
    act_out, gf_out, gw_out,
    outgoing, incoming, code, table, cols, conv, grad, acc, own_tab, hbuf, returned,
    stat_y, stat_x, part, part_in, piece, piece_in,
    h_send, h_recv, sy_send, sy_recv, sx_send, sx_recv, r_send, r_recv,
    wy_send, wy_recv, wx_send, wx_recv,
):
    x, y = lax.axis_index("bx"), lax.axis_index("by")
    rows, channels = feat.shape
    block = rows // 2
    window = send.shape[1] // 2
    slice_y = channels // ny
    slice_x = channels // nx
    groups = piece.shape[1]
    directions = [(i - 1, j - 1) for i in range(3) for j in range(3) if (i, j) != (1, 1)]

    def exists(dx, dy):
        ok = None
        for cond in (
            [x > 0] if dx < 0 else [x < nx - 1] if dx > 0 else []
        ) + ([y > 0] if dy < 0 else [y < ny - 1] if dy > 0 else []):
            ok = cond if ok is None else jnp.logical_and(ok, cond)
        return ok

    def near(dx, dy):
        return (x + dx, y + dy)

    barrier = pltpu.get_barrier_semaphore()
    for d in range(1, ny):
        pl.semaphore_signal(barrier, inc=1, device_id=(x, lax.rem(y + d, ny)), device_id_type=MESH)
    for d in range(1, nx):
        pl.semaphore_signal(barrier, inc=1, device_id=(lax.rem(x + d, nx), y), device_id_type=MESH)
    diagonals = [(dx, dy) for dx, dy in directions if dx and dy]
    for dx, dy in diagonals:
        @pl.when(exists(dx, dy))
        def _(dx=dx, dy=dy):
            pl.semaphore_signal(barrier, inc=1, device_id=near(dx, dy), device_id_type=MESH)

    for s in range(8):
        chosen = jnp.dot(
            row_selector(send[s : s + 1, :], rows), feat[...], preferred_element_type=f32
        ).astype(bf16)
        outgoing[0, s] = chosen[:window]
        outgoing[1, s] = chosen[window:]

    beside_x = (x + nx - 1) // nx + (2 * nx - 2 - x) // nx
    beside_y = (y + ny - 1) // ny + (2 * ny - 2 - y) // ny
    pl.semaphore_wait(barrier, nx + ny - 2 + beside_x * beside_y)

    def halo_copy(s):
        return pltpu.make_async_remote_copy(
            src_ref=outgoing.at[:, s],
            dst_ref=incoming.at[:, 7 - s],
            send_sem=h_send.at[s],
            recv_sem=h_recv.at[7 - s],
            device_id=near(*directions[s]),
            device_id_type=MESH,
        )

    def halo_arrival(s):
        return pltpu.make_async_remote_copy(
            src_ref=outgoing.at[:, s],
            dst_ref=incoming.at[:, s],
            send_sem=h_send.at[s],
            recv_sem=h_recv.at[s],
            device_id=near(*directions[s]),
            device_id_type=MESH,
        )

    for s, (dx, dy) in enumerate(directions):
        @pl.when(exists(dx, dy))
        def _(s=s):
            halo_copy(s).start()

        @pl.when(jnp.logical_not(exists(dx, dy)))
        def _(s=s):
            incoming[:, s] = jnp.zeros((2, window, channels), bf16)
            returned[s] = jnp.zeros((2 * window, channels), bf16)

    entry = nmap[...]
    beyond = entry - rows
    target = beyond // (2 * window)
    inside = lax.rem(beyond, 2 * window)
    inside = jnp.where(inside >= window, inside - window, inside)
    slot = jnp.where(target > 4, target - 1, target)
    far = jnp.where(target == 4, 1023, 1024 + slot * window + inside)
    own = jnp.where(entry >= block, entry - block, entry)
    code[0:OFFSETS, :] = jnp.where(entry < rows, own, far)

    for q in range(2):
        table[q, :, 0:channels] = feat[q * block : (q + 1) * block, :]
    for s, (dx, dy) in enumerate(directions):
        @pl.when(exists(dx, dy))
        def _(s=s):
            halo_arrival(s).wait_recv()
    for q in range(2):
        table[q, :, channels:] = incoming[q].reshape(block, channels)

    for q in range(2):
        lo = q * block

        def gather(g, carry):
            for j in range(GROUP):
                k = g * GROUP + j
                row = code[pl.ds(k, 1), lo : lo + block]
                wide = lanes_from_row(row)
                low = jnp.bitwise_and(wide, 1023)
                lane = lax.broadcasted_iota(jnp.int32, wide.shape, 1)
                pick = jnp.concatenate(
                    [one_hot(low == lane + t) for t in range(0, block, 128)], axis=1
                )
                both = jnp.dot(pick, table[q], preferred_element_type=f32)
                got = jnp.where(wide >= 1024, both[:, channels:], both[:, :channels])
                cols[lo : lo + block, pl.ds(pl.multiple_of(k * 128, 128), 128)] = got.astype(bf16)
            return carry

        lax.fori_loop(0, OFFSETS // GROUP, gather, 0)
        conv[lo : lo + block, :] = jnp.dot(
            cols[lo : lo + block, :], weight[...], preferred_element_type=f32
        ).astype(bf16)

    def spread(buf, r, me, count, peer, send_sems, recv_sems):
        def copy(d, arriving):
            other = lax.rem(me + d, count)
            place = other if arriving else me
            return pltpu.make_async_remote_copy(
                src_ref=buf.at[r, me],
                dst_ref=buf.at[r, place],
                send_sem=send_sems.at[r, other],
                recv_sem=recv_sems.at[r, place],
                device_id=peer(other),
                device_id_type=MESH,
            )

        for d in range(1, count):
            copy(d, False).start()
        for d in range(1, count):
            copy(d, True).wait_recv()
        for d in range(1, count):
            copy(d, False).wait_send()

    def pooled(buf, r, count):
        items = [buf[r, i] for i in range(count)]
        n = functools.reduce(jnp.add, [v[0:1] for v in items])
        s = functools.reduce(jnp.add, [v[1:2] for v in items])
        mean = s / n
        m2 = jnp.zeros_like(s)
        for v in items:
            dev = v[1:2] / v[0:1] - mean
            m2 = m2 + (v[2:3] + v[0:1] * dev * dev)
        return n, s, m2

    along_y = lambda other: (x, other)
    along_x = lambda other: (other, y)

    def put(buf, r, me, *vectors):
        pad = jnp.zeros((8 - len(vectors), channels), f32)
        buf[r, me] = jnp.concatenate(list(vectors) + [pad], axis=0)

    live_rows = live_ref[0, 0]
    live = jnp.where(
        lax.broadcasted_iota(jnp.int32, (rows, channels), 0) < live_rows, 1.0, 0.0
    ).astype(f32)
    values = conv[...].astype(f32)
    n_own = jnp.full((1, channels), live_rows, jnp.int32).astype(f32)
    s_own = jnp.sum(values * live, axis=0, keepdims=True)
    dev = (values - s_own / n_own) * live
    m2_own = jnp.sum(dev * dev, axis=0, keepdims=True)
    put(stat_y, 0, y, n_own, s_own, m2_own)
    spread(stat_y, 0, y, ny, along_y, sy_send, sy_recv)
    put(stat_x, 0, x, *pooled(stat_y, 0, ny))
    spread(stat_x, 0, x, nx, along_x, sx_send, sx_recv)
    total, s_all, m2_all = pooled(stat_x, 0, nx)
    center = s_all / total
    inverse = lax.rsqrt(m2_all / total + epsilon)

    normalized = (values - center) * inverse
    before = gain[...] * normalized + shift[...]
    act_out[...] = (jnp.maximum(before, 0.0) * live).astype(bf16)
    upstream = jnp.where(before > 0.0, cot[...].astype(f32), 0.0) * live
    put(
        stat_y, 1, y,
        jnp.sum(upstream, axis=0, keepdims=True),
        jnp.sum(upstream * normalized, axis=0, keepdims=True),
    )
    spread(stat_y, 1, y, ny, along_y, sy_send, sy_recv)
    stat_x[1, x] = functools.reduce(jnp.add, [stat_y[1, i] for i in range(ny)])
    spread(stat_x, 1, x, nx, along_x, sx_send, sx_recv)
    sums = functools.reduce(jnp.add, [stat_x[1, i] for i in range(nx)])
    sum_up, sum_cross = sums[0:1], sums[1:2]
    conv_grad = (
        gain[...] * inverse * (upstream - live * (sum_up + normalized * sum_cross) / total)
    ).astype(bf16)
    grad[...] = conv_grad

    flipped = conv_grad.astype(f32).T.astype(bf16)
    wide_part = GROUP * 128

    def weight_part(g, carry):
        at = pl.ds(pl.multiple_of(g * wide_part, 128), wide_part)
        term = jnp.dot(flipped, cols[:, at], preferred_element_type=f32).astype(bf16)
        part[:, :, at] = term.reshape(ny, slice_y, wide_part)
        return carry

    lax.fori_loop(0, OFFSETS // GROUP, weight_part, 0)

    def part_copy(d, arriving):
        other = lax.rem(y + d, ny)
        place = other if arriving else y
        return pltpu.make_async_remote_copy(
            src_ref=part.at[other],
            dst_ref=part_in.at[place],
            send_sem=wy_send.at[other],
            recv_sem=wy_recv.at[place],
            device_id=(x, other),
            device_id_type=MESH,
        )

    for d in range(1, ny):
        part_copy(d, False).start()

    def scatter(q):
        lo = q * block
        acc[...] = jnp.zeros_like(acc)

        def step(g, carry):
            at = pl.ds(pl.multiple_of(g * wide_part, 128), wide_part)
            col_grad = lax.dot_general(
                grad[lo : lo + block, :], weight[at, :], (((1,), (1,)), ((), ())),
                preferred_element_type=f32,
            )
            picks, terms = [], []
            place = lax.broadcasted_iota(jnp.int32, (block, block), 0)
            for j in range(GROUP):
                row = code[pl.ds(g * GROUP + j, 1), lo : lo + block]
                picks.append(one_hot(place == jnp.bitwise_and(row, 1023)))
                away = lanes_from_row(row) >= 1024
                term = col_grad[:, j * 128 : (j + 1) * 128]
                terms.append(
                    jnp.concatenate(
                        [jnp.where(away, 0.0, term), jnp.where(away, term, 0.0)], axis=1
                    ).astype(bf16)
                )
            acc[...] += jnp.dot(
                jnp.concatenate(picks, axis=1),
                jnp.concatenate(terms, axis=0),
                preferred_element_type=f32,
            )
            return carry

        lax.fori_loop(0, OFFSETS // GROUP, step, 0)
        own_tab[lo : lo + block, :] = acc[:, 0:channels]
        hbuf[q] = acc[:, channels:].astype(bf16).reshape(8, window, channels)

    def back_copy(q, s, arriving):
        to = s if arriving else 7 - s
        return pltpu.make_async_remote_copy(
            src_ref=hbuf.at[q, s],
            dst_ref=returned.at[to, pl.ds(q * window, window)],
            send_sem=r_send.at[q, s],
            recv_sem=r_recv.at[q, to],
            device_id=near(*directions[s]),
            device_id_type=MESH,
        )

    def send_back(q):
        for s, (dx, dy) in enumerate(directions):
            @pl.when(exists(dx, dy))
            def _(s=s):
                back_copy(q, s, False).start()

    scatter(0)
    send_back(0)

    part_in[y] = part[y]
    for d in range(1, ny):
        part_copy(d, True).wait_recv()
    for g in range(groups):
        strips = []
        for j in range(ny):
            k = g * ny + j
            if k < OFFSETS:
                strip = part_in[:, :, k * 128 : (k + 1) * 128].astype(f32)
                strips.append(jnp.sum(strip, axis=0))
            else:
                strips.append(jnp.zeros((slice_y, 128), f32))
        turned = jnp.concatenate(strips, axis=0).T
        piece[:, g] = turned.reshape(nx, slice_x, channels).astype(bf16)

    def piece_copy(d, arriving):
        other = lax.rem(x + d, nx)
        place = other if arriving else x
        return pltpu.make_async_remote_copy(
            src_ref=piece.at[other],
            dst_ref=piece_in.at[place],
            send_sem=wx_send.at[other],
            recv_sem=wx_recv.at[place],
            device_id=(other, y),
            device_id_type=MESH,
        )

    for d in range(1, nx):
        piece_copy(d, False).start()

    scatter(1)
    send_back(1)

    piece_in[x] = piece[x]
    for d in range(1, nx):
        piece_copy(d, True).wait_recv()
    scale = 1.0 / jnp.sqrt(total)
    for g in range(groups):
        summed = jnp.sum(piece_in[:, g].astype(f32), axis=0) * scale
        for j in range(ny):
            if g * ny + j < OFFSETS:
                gw_out[g * ny + j] = summed[:, j * slice_y : (j + 1) * slice_y]

    for q in range(2):
        for s, (dx, dy) in enumerate(directions):
            @pl.when(exists(dx, dy))
            def _(q=q, s=s):
                back_copy(q, s, True).wait_recv()
    place = lax.broadcasted_iota(jnp.int32, (rows, 2 * window), 0)
    pick = jnp.concatenate([one_hot(place == send[s : s + 1, :]) for s in range(8)], axis=1)
    added = jnp.dot(
        pick, returned[...].reshape(8 * 2 * window, channels), preferred_element_type=f32
    )
    gf_out[...] = (own_tab[...] + added).astype(bf16)

    for s, (dx, dy) in enumerate(directions):
        @pl.when(exists(dx, dy))
        def _(s=s):
            halo_copy(s).wait_send()
            for q in range(2):
                back_copy(q, s, False).wait_send()
    for d in range(1, ny):
        part_copy(d, False).wait_send()
    for d in range(1, nx):
        piece_copy(d, False).wait_send()


def per_device(features, live_count, neighbour_map, send_rows, weight, gain, shift, cotangent):
    nx, ny = lax.axis_size("bx"), lax.axis_size("by")
    rows, channels = features.shape[2:]
    halo = send_rows.shape[3]
    block, window = rows // 2, halo // 2
    slice_x, slice_y = channels // nx, channels // ny
    groups = -(-OFFSETS // ny)
    vmem = pl.BlockSpec(memory_space=pltpu.VMEM)
    dma = pltpu.SemaphoreType.DMA
    activated, grad_features, grad_weight = pl.pallas_call(
        functools.partial(kernel, nx, ny),
        out_shape=(
            jax.ShapeDtypeStruct((rows, channels), bf16),
            jax.ShapeDtypeStruct((rows, channels), bf16),
            jax.ShapeDtypeStruct((OFFSETS, slice_x, slice_y), f32),
        ),
        in_specs=[pl.BlockSpec(memory_space=pltpu.SMEM)] + [vmem] * 7,
        out_specs=(vmem, vmem, vmem),
        scratch_shapes=[
            pltpu.VMEM((2, 8, window, channels), bf16),
            pltpu.VMEM((2, 8, window, channels), bf16),
            pltpu.VMEM((32, rows), jnp.int32),
            pltpu.VMEM((2, block, 2 * channels), bf16),
            pltpu.VMEM((rows, OFFSETS * channels), bf16),
            pltpu.VMEM((rows, channels), bf16),
            pltpu.VMEM((rows, channels), bf16),
            pltpu.VMEM((block, 2 * channels), f32),
            pltpu.VMEM((rows, channels), f32),
            pltpu.VMEM((2, 8, window, channels), bf16),
            pltpu.VMEM((8, halo, channels), bf16),
            pltpu.VMEM((2, ny, 8, channels), f32),
            pltpu.VMEM((2, nx, 8, channels), f32),
            pltpu.VMEM((ny, slice_y, OFFSETS * channels), bf16),
            pltpu.VMEM((ny, slice_y, OFFSETS * channels), bf16),
            pltpu.VMEM((nx, groups, slice_x, channels), bf16),
            pltpu.VMEM((nx, groups, slice_x, channels), bf16),
            dma((8,)), dma((8,)),
            dma((2, ny)), dma((2, ny)),
            dma((2, nx)), dma((2, nx)),
            dma((2, 8)), dma((2, 8)),
            dma((ny,)), dma((ny,)),
            dma((nx,)), dma((nx,)),
        ],
        compiler_params=pltpu.CompilerParams(
            collective_id=0, has_side_effects=True, vmem_limit_bytes=48 * 1024 * 1024
        ),
    )(
        live_count,
        features[0, 0],
        neighbour_map[0, 0],
        send_rows[0, 0],
        weight,
        gain.reshape(1, -1),
        shift.reshape(1, -1),
        cotangent[0, 0],
    )
    return activated[None, None], grad_features[None, None], grad_weight


def solution(mesh):
    return jax.shard_map(
        per_device,
        mesh=mesh,
        in_specs=(
            P("bx", "by", None, None),
            P("bx", "by"),
            P("bx", "by", None, None),
            P("bx", "by", None, None),
            P(),
            P(),
            P(),
            P("bx", "by", None, None),
        ),
        out_specs=(P("bx", "by", None, None), P("bx", "by", None, None), P(None, "bx", "by")),
        check_vma=False,
    )
```

```python
import functools

import jax
import jax.numpy as jnp
from jax import lax
from jax.experimental import pallas as pl
from jax.experimental.pallas import tpu as pltpu
from jax.sharding import PartitionSpec as P

epsilon = 1e-05
OFFSETS = 27
GROUP = 3
MESH = pl.DeviceIdType.MESH
f32 = jnp.float32
bf16 = jnp.bfloat16


def lanes_from_row(row):
    return jnp.broadcast_to(row, (128, row.shape[1])).T


def hot16(mask):
    return jnp.where(mask, jnp.ones((), bf16), jnp.zeros((), bf16))


def along_lanes(wide, width):
    n = wide.shape[0]
    wide = wide.astype(jnp.int16).reshape(n // 16, 16, 128)
    lane = lax.broadcasted_iota(jnp.int32, (1, 16, 128), 2).astype(jnp.int16)
    parts = [hot16(wide == lane + jnp.int16(t)).reshape(n, 128) for t in range(0, width, 128)]
    return jnp.concatenate(parts, axis=1)


def along_rows(row, width):
    place = lax.broadcasted_iota(jnp.int32, (width, 128), 0).astype(jnp.int16)
    row = jnp.broadcast_to(row, (16, row.shape[1])).astype(jnp.int16)
    parts = []
    for t in range(0, row.shape[1], 128):
        piece = row[:, t : t + 128]
        parts.append(
            hot16(place.reshape(width // 16, 16, 128) == piece[None]).reshape(width, 128)
        )
    return jnp.concatenate(parts, axis=1)


def row_selector(row, width):
    return along_lanes(lanes_from_row(row), width)


def kernel(
    nx, ny, live_ref, feat_in, nmap_in, send_in, weight_in, gain, shift, cot_in,
    act_out, gf_out, gw_out,
    feat, nmap, send, weight, cot, picks,
    outgoing, incoming, code, table, cols, conv, grad, acc, own_tab, hbuf, returned,
    stat_y, stat_x, part, part_in, piece, piece_in,
    h_send, h_recv, sy_send, sy_recv, sx_send, sx_recv, r_send, r_recv,
    wy_send, wy_recv, wx_send, wx_recv, in_sems,
):
    x, y = lax.axis_index("bx"), lax.axis_index("by")
    rows, channels = feat.shape
    block = rows // 2
    window = send.shape[1] // 2
    slice_y = channels // ny
    slice_x = channels // nx
    groups = piece.shape[1]
    directions = [(i - 1, j - 1) for i in range(3) for j in range(3) if (i, j) != (1, 1)]

    def exists(dx, dy):
        ok = None
        for cond in (
            [x > 0] if dx < 0 else [x < nx - 1] if dx > 0 else []
        ) + ([y > 0] if dy < 0 else [y < ny - 1] if dy > 0 else []):
            ok = cond if ok is None else jnp.logical_and(ok, cond)
        return ok

    def near(dx, dy):
        return (x + dx, y + dy)

    loads = [
        pltpu.make_async_copy(src, dst, in_sems.at[i])
        for i, (src, dst) in enumerate(
            [(send_in, send), (feat_in, feat), (nmap_in, nmap), (weight_in, weight), (cot_in, cot)]
        )
    ]
    for load in loads:
        load.start()

    barrier = pltpu.get_barrier_semaphore()
    for d in range(1, ny):
        pl.semaphore_signal(barrier, inc=1, device_id=(x, lax.rem(y + d, ny)), device_id_type=MESH)
    for d in range(1, nx):
        pl.semaphore_signal(barrier, inc=1, device_id=(lax.rem(x + d, nx), y), device_id_type=MESH)
    diagonals = [(dx, dy) for dx, dy in directions if dx and dy]
    for dx, dy in diagonals:
        @pl.when(exists(dx, dy))
        def _(dx=dx, dy=dy):
            pl.semaphore_signal(barrier, inc=1, device_id=near(dx, dy), device_id_type=MESH)

    loads[0].wait()
    loads[1].wait()
    for s in range(8):
        chosen = jnp.dot(
            row_selector(send[s : s + 1, :], rows), feat[...], preferred_element_type=f32
        ).astype(bf16)
        outgoing[0, s] = chosen[:window]
        outgoing[1, s] = chosen[window:]

    beside_x = (x + nx - 1) // nx + (2 * nx - 2 - x) // nx
    beside_y = (y + ny - 1) // ny + (2 * ny - 2 - y) // ny
    pl.semaphore_wait(barrier, nx + ny - 2 + beside_x * beside_y)

    def halo_copy(s):
        return pltpu.make_async_remote_copy(
            src_ref=outgoing.at[:, s],
            dst_ref=incoming.at[:, 7 - s],
            send_sem=h_send.at[s],
            recv_sem=h_recv.at[7 - s],
            device_id=near(*directions[s]),
            device_id_type=MESH,
        )

    def halo_arrival(s):
        return pltpu.make_async_remote_copy(
            src_ref=outgoing.at[:, s],
            dst_ref=incoming.at[:, s],
            send_sem=h_send.at[s],
            recv_sem=h_recv.at[s],
            device_id=near(*directions[s]),
            device_id_type=MESH,
        )

    for s, (dx, dy) in enumerate(directions):
        @pl.when(exists(dx, dy))
        def _(s=s):
            halo_copy(s).start()

        @pl.when(jnp.logical_not(exists(dx, dy)))
        def _(s=s):
            incoming[:, s] = jnp.zeros((2, window, channels), bf16)
            returned[s] = jnp.zeros((2 * window, channels), bf16)

    loads[2].wait()
    entry = nmap[...]
    beyond = entry - rows
    target = beyond // (2 * window)
    inside = lax.rem(beyond, 2 * window)
    inside = jnp.where(inside >= window, inside - window, inside)
    slot = jnp.where(target > 4, target - 1, target)
    far = jnp.where(target == 4, 1023, 1024 + slot * window + inside)
    own = jnp.where(entry >= block, entry - block, entry)
    code[0:OFFSETS, :] = jnp.where(entry < rows, own, far)

    def make_picks(first, last):
        def one(k, carry):
            for q in range(2):
                row = jnp.bitwise_and(code[pl.ds(k, 1), q * block : (q + 1) * block], 1023)
                at = pl.ds(pl.multiple_of(k * block, 128), block)
                picks[q, :, at] = along_rows(row, block)
            return carry

        lax.fori_loop(first, last, one, 0)

    make_picks(0, 9)

    for q in range(2):
        table[q, :, 0:channels] = feat[q * block : (q + 1) * block, :]
    for s, (dx, dy) in enumerate(directions):
        @pl.when(exists(dx, dy))
        def _(s=s):
            halo_arrival(s).wait_recv()
    for q in range(2):
        table[q, :, channels:] = incoming[q].reshape(block, channels)

    loads[3].wait()
    for q in range(2):
        lo = q * block

        def gather(g, carry):
            for j in range(GROUP):
                k = g * GROUP + j
                row = code[pl.ds(k, 1), lo : lo + block]
                wide = lanes_from_row(row)
                pick = along_lanes(jnp.bitwise_and(wide, 1023), block)
                both = jnp.dot(pick, table[q], preferred_element_type=f32)
                got = jnp.where(wide >= 1024, both[:, channels:], both[:, :channels])
                cols[lo : lo + block, pl.ds(pl.multiple_of(k * 128, 128), 128)] = got.astype(bf16)
            return carry

        lax.fori_loop(0, OFFSETS // GROUP, gather, 0)
        conv[lo : lo + block, :] = jnp.dot(
            cols[lo : lo + block, :], weight[...], preferred_element_type=f32
        ).astype(bf16)

    def spread(buf, r, me, count, peer, send_sems, recv_sems, meanwhile):
        def copy(d, arriving):
            other = lax.rem(me + d, count)
            place = other if arriving else me
            return pltpu.make_async_remote_copy(
                src_ref=buf.at[r, me],
                dst_ref=buf.at[r, place],
                send_sem=send_sems.at[r, other],
                recv_sem=recv_sems.at[r, place],
                device_id=peer(other),
                device_id_type=MESH,
            )

        for d in range(1, count):
            copy(d, False).start()
        make_picks(*meanwhile)
        for d in range(1, count):
            copy(d, True).wait_recv()
        for d in range(1, count):
            copy(d, False).wait_send()

    def pooled(buf, r, count):
        items = [buf[r, i] for i in range(count)]
        n = functools.reduce(jnp.add, [v[0:1] for v in items])
        s = functools.reduce(jnp.add, [v[1:2] for v in items])
        mean = s / n
        m2 = jnp.zeros_like(s)
        for v in items:
            dev = v[1:2] / v[0:1] - mean
            m2 = m2 + (v[2:3] + v[0:1] * dev * dev)
        return n, s, m2

    along_y = lambda other: (x, other)
    along_x = lambda other: (other, y)

    def put(buf, r, me, *vectors):
        pad = jnp.zeros((8 - len(vectors), channels), f32)
        buf[r, me] = jnp.concatenate(list(vectors) + [pad], axis=0)

    live_rows = live_ref[0, 0]
    live = jnp.where(
        lax.broadcasted_iota(jnp.int32, (rows, channels), 0) < live_rows, 1.0, 0.0
    ).astype(f32)
    values = conv[...].astype(f32)
    n_own = jnp.full((1, channels), live_rows, jnp.int32).astype(f32)
    s_own = jnp.sum(values * live, axis=0, keepdims=True)
    dev = (values - s_own / n_own) * live
    m2_own = jnp.sum(dev * dev, axis=0, keepdims=True)
    put(stat_y, 0, y, n_own, s_own, m2_own)
    spread(stat_y, 0, y, ny, along_y, sy_send, sy_recv, (9, 13))
    put(stat_x, 0, x, *pooled(stat_y, 0, ny))
    spread(stat_x, 0, x, nx, along_x, sx_send, sx_recv, (13, 18))
    total, s_all, m2_all = pooled(stat_x, 0, nx)
    center = s_all / total
    inverse = lax.rsqrt(m2_all / total + epsilon)

    loads[4].wait()
    normalized = (values - center) * inverse
    before = gain[...] * normalized + shift[...]
    act_out[...] = (jnp.maximum(before, 0.0) * live).astype(bf16)
    upstream = jnp.where(before > 0.0, cot[...].astype(f32), 0.0) * live
    put(
        stat_y, 1, y,
        jnp.sum(upstream, axis=0, keepdims=True),
        jnp.sum(upstream * normalized, axis=0, keepdims=True),
    )
    spread(stat_y, 1, y, ny, along_y, sy_send, sy_recv, (18, 22))
    stat_x[1, x] = functools.reduce(jnp.add, [stat_y[1, i] for i in range(ny)])
    spread(stat_x, 1, x, nx, along_x, sx_send, sx_recv, (22, 27))
    sums = functools.reduce(jnp.add, [stat_x[1, i] for i in range(nx)])
    sum_up, sum_cross = sums[0:1], sums[1:2]
    conv_grad = (
        gain[...] * inverse * (upstream - live * (sum_up + normalized * sum_cross) / total)
    ).astype(bf16)
    grad[...] = conv_grad

    flipped = conv_grad.astype(f32).T.astype(bf16)
    wide_part = GROUP * 128

    def weight_part(g, carry):
        at = pl.ds(pl.multiple_of(g * wide_part, 128), wide_part)
        term = jnp.dot(flipped, cols[:, at], preferred_element_type=f32).astype(bf16)
        part[:, :, at] = term.reshape(ny, slice_y, wide_part)
        return carry

    lax.fori_loop(0, OFFSETS // GROUP, weight_part, 0)

    def part_copy(d, arriving):
        other = lax.rem(y + d, ny)
        place = other if arriving else y
        return pltpu.make_async_remote_copy(
            src_ref=part.at[other],
            dst_ref=part_in.at[place],
            send_sem=wy_send.at[other],
            recv_sem=wy_recv.at[place],
            device_id=(x, other),
            device_id_type=MESH,
        )

    for d in range(1, ny):
        part_copy(d, False).start()

    def scatter(q):
        lo = q * block
        acc[...] = jnp.zeros_like(acc)

        def step(g, carry):
            at = pl.ds(pl.multiple_of(g * wide_part, 128), wide_part)
            col_grad = lax.dot_general(
                grad[lo : lo + block, :], weight[at, :], (((1,), (1,)), ((), ())),
                preferred_element_type=f32,
            )
            terms = []
            chosen_at = pl.ds(pl.multiple_of(g * GROUP * block, 128), GROUP * block)
            for j in range(GROUP):
                row = code[pl.ds(g * GROUP + j, 1), lo : lo + block]
                away = lanes_from_row(row) >= 1024
                term = col_grad[:, j * 128 : (j + 1) * 128]
                terms.append(
                    jnp.concatenate(
                        [jnp.where(away, 0.0, term), jnp.where(away, term, 0.0)], axis=1
                    ).astype(bf16)
                )
            acc[...] += jnp.dot(
                picks[q, :, chosen_at],
                jnp.concatenate(terms, axis=0),
                preferred_element_type=f32,
            )
            return carry

        lax.fori_loop(0, OFFSETS // GROUP, step, 0)
        own_tab[lo : lo + block, :] = acc[:, 0:channels]
        hbuf[q] = acc[:, channels:].astype(bf16).reshape(8, window, channels)

    def back_copy(q, s, arriving):
        to = s if arriving else 7 - s
        return pltpu.make_async_remote_copy(
            src_ref=hbuf.at[q, s],
            dst_ref=returned.at[to, pl.ds(q * window, window)],
            send_sem=r_send.at[q, s],
            recv_sem=r_recv.at[q, to],
            device_id=near(*directions[s]),
            device_id_type=MESH,
        )

    def send_back(q):
        for s, (dx, dy) in enumerate(directions):
            @pl.when(exists(dx, dy))
            def _(s=s):
                back_copy(q, s, False).start()

    scatter(0)
    send_back(0)

    part_in[y] = part[y]
    for d in range(1, ny):
        part_copy(d, True).wait_recv()
    for g in range(groups):
        strips = []
        for j in range(ny):
            k = g * ny + j
            if k < OFFSETS:
                strip = part_in[:, :, k * 128 : (k + 1) * 128].astype(f32)
                strips.append(jnp.sum(strip, axis=0))
            else:
                strips.append(jnp.zeros((slice_y, 128), f32))
        turned = jnp.concatenate(strips, axis=0).T
        piece[:, g] = turned.reshape(nx, slice_x, channels).astype(bf16)

    def piece_copy(d, arriving):
        other = lax.rem(x + d, nx)
        place = other if arriving else x
        return pltpu.make_async_remote_copy(
            src_ref=piece.at[other],
            dst_ref=piece_in.at[place],
            send_sem=wx_send.at[other],
            recv_sem=wx_recv.at[place],
            device_id=(other, y),
            device_id_type=MESH,
        )

    for d in range(1, nx):
        piece_copy(d, False).start()

    scatter(1)
    send_back(1)

    piece_in[x] = piece[x]
    for d in range(1, nx):
        piece_copy(d, True).wait_recv()
    scale = 1.0 / jnp.sqrt(total)
    for g in range(groups):
        summed = jnp.sum(piece_in[:, g].astype(f32), axis=0) * scale
        for j in range(ny):
            if g * ny + j < OFFSETS:
                gw_out[g * ny + j] = summed[:, j * slice_y : (j + 1) * slice_y]

    for q in range(2):
        for s, (dx, dy) in enumerate(directions):
            @pl.when(exists(dx, dy))
            def _(q=q, s=s):
                back_copy(q, s, True).wait_recv()
    pick = jnp.concatenate([along_rows(send[s : s + 1, :], rows) for s in range(8)], axis=1)
    added = jnp.dot(
        pick, returned[...].reshape(8 * 2 * window, channels), preferred_element_type=f32
    )
    gf_out[...] = (own_tab[...] + added).astype(bf16)

    for s, (dx, dy) in enumerate(directions):
        @pl.when(exists(dx, dy))
        def _(s=s):
            halo_copy(s).wait_send()
            for q in range(2):
                back_copy(q, s, False).wait_send()
    for d in range(1, ny):
        part_copy(d, False).wait_send()
    for d in range(1, nx):
        piece_copy(d, False).wait_send()


def per_device(features, live_count, neighbour_map, send_rows, weight, gain, shift, cotangent):
    nx, ny = lax.axis_size("bx"), lax.axis_size("by")
    rows, channels = features.shape[2:]
    halo = send_rows.shape[3]
    block, window = rows // 2, halo // 2
    slice_x, slice_y = channels // nx, channels // ny
    groups = -(-OFFSETS // ny)
    vmem = pl.BlockSpec(memory_space=pltpu.VMEM)
    hbm = pl.BlockSpec(memory_space=pltpu.HBM)
    dma = pltpu.SemaphoreType.DMA
    activated, grad_features, grad_weight = pl.pallas_call(
        functools.partial(kernel, nx, ny),
        out_shape=(
            jax.ShapeDtypeStruct((rows, channels), bf16),
            jax.ShapeDtypeStruct((rows, channels), bf16),
            jax.ShapeDtypeStruct((OFFSETS, slice_x, slice_y), f32),
        ),
        in_specs=[
            pl.BlockSpec(memory_space=pltpu.SMEM), hbm, hbm, hbm, hbm, vmem, vmem, hbm,
        ],
        out_specs=(vmem, vmem, vmem),
        scratch_shapes=[
            pltpu.VMEM((rows, channels), bf16),
            pltpu.VMEM((OFFSETS, rows), jnp.int32),
            pltpu.VMEM((8, halo), jnp.int32),
            pltpu.VMEM((OFFSETS * channels, channels), bf16),
            pltpu.VMEM((rows, channels), bf16),
            pltpu.VMEM((2, block, OFFSETS * block), bf16),
            pltpu.VMEM((2, 8, window, channels), bf16),
            pltpu.VMEM((2, 8, window, channels), bf16),
            pltpu.VMEM((32, rows), jnp.int32),
            pltpu.VMEM((2, block, 2 * channels), bf16),
            pltpu.VMEM((rows, OFFSETS * channels), bf16),
            pltpu.VMEM((rows, channels), bf16),
            pltpu.VMEM((rows, channels), bf16),
            pltpu.VMEM((block, 2 * channels), f32),
            pltpu.VMEM((rows, channels), f32),
            pltpu.VMEM((2, 8, window, channels), bf16),
            pltpu.VMEM((8, halo, channels), bf16),
            pltpu.VMEM((2, ny, 8, channels), f32),
            pltpu.VMEM((2, nx, 8, channels), f32),
            pltpu.VMEM((ny, slice_y, OFFSETS * channels), bf16),
            pltpu.VMEM((ny, slice_y, OFFSETS * channels), bf16),
            pltpu.VMEM((nx, groups, slice_x, channels), bf16),
            pltpu.VMEM((nx, groups, slice_x, channels), bf16),
            dma((8,)), dma((8,)),
            dma((2, ny)), dma((2, ny)),
            dma((2, nx)), dma((2, nx)),
            dma((2, 8)), dma((2, 8)),
            dma((ny,)), dma((ny,)),
            dma((nx,)), dma((nx,)),
            dma((5,)),
        ],
        compiler_params=pltpu.CompilerParams(
            collective_id=0, has_side_effects=True, vmem_limit_bytes=58 * 1024 * 1024
        ),
    )(
        live_count,
        features[0, 0],
        neighbour_map[0, 0],
        send_rows[0, 0],
        weight,
        gain.reshape(1, -1),
        shift.reshape(1, -1),
        cotangent[0, 0],
    )
    return activated[None, None], grad_features[None, None], grad_weight


def solution(mesh):
    return jax.shard_map(
        per_device,
        mesh=mesh,
        in_specs=(
            P("bx", "by", None, None),
            P("bx", "by"),
            P("bx", "by", None, None),
            P("bx", "by", None, None),
            P(),
            P(),
            P(),
            P("bx", "by", None, None),
        ),
        out_specs=(P("bx", "by", None, None), P("bx", "by", None, None), P(None, "bx", "by")),
        check_vma=False,
    )
```

```python
import functools

import jax
import jax.numpy as jnp
from jax import lax
from jax.experimental import pallas as pl
from jax.experimental.pallas import tpu as pltpu
from jax.sharding import PartitionSpec as P

epsilon = 1e-05
OFFSETS = 27
GROUP = 3
WIDE_GROUP = 9
MESH = pl.DeviceIdType.MESH
f32 = jnp.float32
bf16 = jnp.bfloat16


def lanes_from_row(row):
    return jnp.broadcast_to(row, (128, row.shape[1])).T


def hot16(mask):
    return jnp.where(mask, jnp.ones((), bf16), jnp.zeros((), bf16))


def along_lanes(wide, width):
    n = wide.shape[0]
    wide = wide.astype(jnp.int16).reshape(n // 16, 16, 128)
    lane = lax.broadcasted_iota(jnp.int32, (1, 16, 128), 2).astype(jnp.int16)
    parts = [hot16(wide == lane + jnp.int16(t)).reshape(n, 128) for t in range(0, width, 128)]
    return jnp.concatenate(parts, axis=1)


def along_rows(row, width):
    place = lax.broadcasted_iota(jnp.int32, (width, 128), 0).astype(jnp.int16)
    row = jnp.broadcast_to(row, (16, row.shape[1])).astype(jnp.int16)
    parts = []
    for t in range(0, row.shape[1], 128):
        piece = row[:, t : t + 128]
        parts.append(
            hot16(place.reshape(width // 16, 16, 128) == piece[None]).reshape(width, 128)
        )
    return jnp.concatenate(parts, axis=1)


def row_selector(row, width):
    return along_lanes(lanes_from_row(row), width)


def kernel(
    nx, ny, live_ref, feat_in, nmap_in, send_in, weight_in, gain, shift, cot_in,
    act_out, gf_out, gw_out,
    feat, nmap, send, weight, cot, picks,
    outgoing, incoming, code, code_t, table, cols, conv, grad, acc, own_tab, hbuf, returned,
    stat_y, stat_x, part, mate_in, pair_out, part_in, piece, piece_in,
    h_send, h_recv, sy_send, sy_recv, sx_send, sx_recv, r_send, r_recv,
    wm_send, wm_recv, wy_send, wy_recv, wx_send, wx_recv, in_sems,
):
    x, y = lax.axis_index("bx"), lax.axis_index("by")
    rows, channels = feat.shape
    block = rows // 2
    window = send.shape[1] // 2
    slice_y = channels // ny
    slice_x = channels // nx
    groups = piece.shape[1]
    directions = [(i - 1, j - 1) for i in range(3) for j in range(3) if (i, j) != (1, 1)]

    def exists(dx, dy):
        ok = None
        for cond in (
            [x > 0] if dx < 0 else [x < nx - 1] if dx > 0 else []
        ) + ([y > 0] if dy < 0 else [y < ny - 1] if dy > 0 else []):
            ok = cond if ok is None else jnp.logical_and(ok, cond)
        return ok

    def near(dx, dy):
        return (x + dx, y + dy)

    loads = [
        pltpu.make_async_copy(src, dst, in_sems.at[i])
        for i, (src, dst) in enumerate(
            [(send_in, send), (feat_in, feat), (nmap_in, nmap), (weight_in, weight), (cot_in, cot)]
        )
    ]
    for load in loads:
        load.start()

    barrier = pltpu.get_barrier_semaphore()
    for d in range(1, ny):
        pl.semaphore_signal(barrier, inc=1, device_id=(x, lax.rem(y + d, ny)), device_id_type=MESH)
    for d in range(1, nx):
        pl.semaphore_signal(barrier, inc=1, device_id=(lax.rem(x + d, nx), y), device_id_type=MESH)
    diagonals = [(dx, dy) for dx, dy in directions if dx and dy]
    for dx, dy in diagonals:
        @pl.when(exists(dx, dy))
        def _(dx=dx, dy=dy):
            pl.semaphore_signal(barrier, inc=1, device_id=near(dx, dy), device_id_type=MESH)

    loads[0].wait()
    loads[1].wait()
    for s in range(8):
        chosen = jnp.dot(
            row_selector(send[s : s + 1, :], rows), feat[...], preferred_element_type=f32
        ).astype(bf16)
        outgoing[0, s] = chosen[:window]
        outgoing[1, s] = chosen[window:]

    beside_x = (x + nx - 1) // nx + (2 * nx - 2 - x) // nx
    beside_y = (y + ny - 1) // ny + (2 * ny - 2 - y) // ny
    pl.semaphore_wait(barrier, nx + ny - 2 + beside_x * beside_y)

    def halo_copy(s):
        return pltpu.make_async_remote_copy(
            src_ref=outgoing.at[:, s],
            dst_ref=incoming.at[:, 7 - s],
            send_sem=h_send.at[s],
            recv_sem=h_recv.at[7 - s],
            device_id=near(*directions[s]),
            device_id_type=MESH,
        )

    def halo_arrival(s):
        return pltpu.make_async_remote_copy(
            src_ref=outgoing.at[:, s],
            dst_ref=incoming.at[:, s],
            send_sem=h_send.at[s],
            recv_sem=h_recv.at[s],
            device_id=near(*directions[s]),
            device_id_type=MESH,
        )

    for s, (dx, dy) in enumerate(directions):
        @pl.when(exists(dx, dy))
        def _(s=s):
            halo_copy(s).start()

        @pl.when(jnp.logical_not(exists(dx, dy)))
        def _(s=s):
            incoming[:, s] = jnp.zeros((2, window, channels), bf16)
            returned[s] = jnp.zeros((2 * window, channels), bf16)

    loads[2].wait()
    entry = nmap[...]
    beyond = entry - rows
    target = beyond // (2 * window)
    inside = lax.rem(beyond, 2 * window)
    inside = jnp.where(inside >= window, inside - window, inside)
    slot = jnp.where(target > 4, target - 1, target)
    far = jnp.where(target == 4, 1023, 1024 + slot * window + inside)
    own = jnp.where(entry >= block, entry - block, entry)
    coded = jnp.where(entry < rows, own, far)
    coded = coded.reshape(OFFSETS, rows // 128, 128)
    for i in range(rows // 128):
        code[0:OFFSETS, i * 128 : (i + 1) * 128] = coded[:, i, :]
    code[OFFSETS:, :] = jnp.zeros((32 - OFFSETS, rows), jnp.int32)
    code_t[...] = jnp.concatenate([code[...], jnp.zeros((96, rows), jnp.int32)], axis=0).T

    def columns_from(lo, first):
        turn = lax.rem(128 - first, 128)
        return pltpu.roll(code_t[lo : lo + block, :], turn, axis=1)

    def make_picks(first, last):
        def one(k, carry):
            for q in range(2):
                row = jnp.bitwise_and(code[pl.ds(k, 1), q * block : (q + 1) * block], 1023)
                at = pl.ds(pl.multiple_of(k * block, 128), block)
                picks[q, :, at] = along_rows(row, block)
            return carry

        lax.fori_loop(first, last, one, 0)

    make_picks(0, 9)

    for q in range(2):
        table[q, :, 0:channels] = feat[q * block : (q + 1) * block, :]
    for s, (dx, dy) in enumerate(directions):
        @pl.when(exists(dx, dy))
        def _(s=s):
            halo_arrival(s).wait_recv()
    for q in range(2):
        table[q, :, channels:] = incoming[q].reshape(block, channels)

    loads[3].wait()
    for q in range(2):
        lo = q * block

        def gather(g, carry):
            turned = columns_from(lo, g * WIDE_GROUP)
            for j in range(WIDE_GROUP):
                k = g * WIDE_GROUP + j
                wide = jnp.broadcast_to(turned[:, j : j + 1], (block, 128))
                pick = along_lanes(jnp.bitwise_and(wide, 1023), block)
                both = jnp.dot(pick, table[q], preferred_element_type=f32)
                got = jnp.where(wide >= 1024, both[:, channels:], both[:, :channels])
                cols[lo : lo + block, pl.ds(pl.multiple_of(k * 128, 128), 128)] = got.astype(bf16)
            return carry

        lax.fori_loop(0, OFFSETS // WIDE_GROUP, gather, 0)
        conv[lo : lo + block, :] = jnp.dot(
            cols[lo : lo + block, :], weight[...], preferred_element_type=f32
        ).astype(bf16)

    def spread(buf, r, me, count, peer, send_sems, recv_sems, meanwhile):
        def copy(d, arriving):
            other = lax.rem(me + d, count)
            place = other if arriving else me
            return pltpu.make_async_remote_copy(
                src_ref=buf.at[r, me],
                dst_ref=buf.at[r, place],
                send_sem=send_sems.at[r, other],
                recv_sem=recv_sems.at[r, place],
                device_id=peer(other),
                device_id_type=MESH,
            )

        for d in range(1, count):
            copy(d, False).start()
        make_picks(*meanwhile)
        for d in range(1, count):
            copy(d, True).wait_recv()
        for d in range(1, count):
            copy(d, False).wait_send()

    def pooled(buf, r, count):
        items = [buf[r, i] for i in range(count)]
        n = functools.reduce(jnp.add, [v[0:1] for v in items])
        s = functools.reduce(jnp.add, [v[1:2] for v in items])
        mean = s / n
        m2 = jnp.zeros_like(s)
        for v in items:
            dev = v[1:2] / v[0:1] - mean
            m2 = m2 + (v[2:3] + v[0:1] * dev * dev)
        return n, s, m2

    along_y = lambda other: (x, other)
    along_x = lambda other: (other, y)

    def put(buf, r, me, *vectors):
        pad = jnp.zeros((8 - len(vectors), channels), f32)
        buf[r, me] = jnp.concatenate(list(vectors) + [pad], axis=0)

    live_rows = live_ref[0, 0]
    live = jnp.where(
        lax.broadcasted_iota(jnp.int32, (rows, channels), 0) < live_rows, 1.0, 0.0
    ).astype(f32)
    values = conv[...].astype(f32)
    n_own = jnp.full((1, channels), live_rows, jnp.int32).astype(f32)
    s_own = jnp.sum(values * live, axis=0, keepdims=True)
    dev = (values - s_own / n_own) * live
    m2_own = jnp.sum(dev * dev, axis=0, keepdims=True)
    put(stat_y, 0, y, n_own, s_own, m2_own)
    spread(stat_y, 0, y, ny, along_y, sy_send, sy_recv, (9, 13))
    put(stat_x, 0, x, *pooled(stat_y, 0, ny))
    spread(stat_x, 0, x, nx, along_x, sx_send, sx_recv, (13, 18))
    total, s_all, m2_all = pooled(stat_x, 0, nx)
    center = s_all / total
    inverse = lax.rsqrt(m2_all / total + epsilon)

    loads[4].wait()
    normalized = (values - center) * inverse
    before = gain[...] * normalized + shift[...]
    act_out[...] = (jnp.maximum(before, 0.0) * live).astype(bf16)
    upstream = jnp.where(before > 0.0, cot[...].astype(f32), 0.0) * live
    put(
        stat_y, 1, y,
        jnp.sum(upstream, axis=0, keepdims=True),
        jnp.sum(upstream * normalized, axis=0, keepdims=True),
    )
    spread(stat_y, 1, y, ny, along_y, sy_send, sy_recv, (18, 22))
    stat_x[1, x] = functools.reduce(jnp.add, [stat_y[1, i] for i in range(ny)])
    spread(stat_x, 1, x, nx, along_x, sx_send, sx_recv, (22, 27))
    sums = functools.reduce(jnp.add, [stat_x[1, i] for i in range(nx)])
    sum_up, sum_cross = sums[0:1], sums[1:2]
    conv_grad = (
        gain[...] * inverse * (upstream - live * (sum_up + normalized * sum_cross) / total)
    ).astype(bf16)
    grad[...] = conv_grad

    flipped = conv_grad.astype(f32).T.astype(bf16)
    wide_part = GROUP * 128

    def weight_part(g, carry):
        at = pl.ds(pl.multiple_of(g * wide_part, 128), wide_part)
        term = jnp.dot(flipped, cols[:, at], preferred_element_type=f32).astype(bf16)
        term = term.reshape(ny, slice_y, wide_part)
        for i in range(ny):
            part[i % 2, i // 2, :, at] = term[i]
        return carry

    lax.fori_loop(0, OFFSETS // GROUP, weight_part, 0)

    half = ny // 2
    mine, pair = lax.rem(y, 2), y // 2
    mate = y + 1 - 2 * mine

    def mate_copy():
        return pltpu.make_async_remote_copy(
            src_ref=part.at[1 - mine],
            dst_ref=mate_in,
            send_sem=wm_send.at[0],
            recv_sem=wm_recv.at[0],
            device_id=(x, mate),
            device_id_type=MESH,
        )

    mate_copy().start()

    def pair_copy(d, arriving):
        other = lax.rem(pair + d, half)
        place = other if arriving else pair
        return pltpu.make_async_remote_copy(
            src_ref=pair_out.at[other],
            dst_ref=part_in.at[place],
            send_sem=wy_send.at[other],
            recv_sem=wy_recv.at[place],
            device_id=(x, 2 * other + mine),
            device_id_type=MESH,
        )

    steps = OFFSETS // GROUP

    def scatter(q, first, last):
        lo = q * block
        if first == 0:
            acc[...] = jnp.zeros_like(acc)

        def step(g, carry):
            at = pl.ds(pl.multiple_of(g * wide_part, 128), wide_part)
            col_grad = lax.dot_general(
                grad[lo : lo + block, :], weight[at, :], (((1,), (1,)), ((), ())),
                preferred_element_type=f32,
            )
            terms = []
            turned = columns_from(lo, g * GROUP)
            chosen_at = pl.ds(pl.multiple_of(g * GROUP * block, 128), GROUP * block)
            for j in range(GROUP):
                away = jnp.broadcast_to(turned[:, j : j + 1], (block, 128)) >= 1024
                term = col_grad[:, j * 128 : (j + 1) * 128]
                terms.append(
                    jnp.concatenate(
                        [jnp.where(away, 0.0, term), jnp.where(away, term, 0.0)], axis=1
                    ).astype(bf16)
                )
            acc[...] += jnp.dot(
                picks[q, :, chosen_at],
                jnp.concatenate(terms, axis=0),
                preferred_element_type=f32,
            )
            return carry

        lax.fori_loop(first, last, step, 0)
        if last < steps:
            return
        own_tab[lo : lo + block, :] = acc[:, 0:channels]
        hbuf[q] = acc[:, channels:].astype(bf16).reshape(8, window, channels)

    def back_copy(q, s, arriving):
        to = s if arriving else 7 - s
        return pltpu.make_async_remote_copy(
            src_ref=hbuf.at[q, s],
            dst_ref=returned.at[to, pl.ds(q * window, window)],
            send_sem=r_send.at[q, s],
            recv_sem=r_recv.at[q, to],
            device_id=near(*directions[s]),
            device_id_type=MESH,
        )

    def send_back(q):
        for s, (dx, dy) in enumerate(directions):
            @pl.when(exists(dx, dy))
            def _(s=s):
                back_copy(q, s, False).start()

    scatter(0, 0, 3)
    mate_copy().wait_recv()
    pair_out[...] = (part[mine].astype(f32) + mate_in[...].astype(f32)).astype(bf16)
    for d in range(1, half):
        pair_copy(d, False).start()
    scatter(0, 3, steps)
    send_back(0)
    scatter(1, 0, 2)

    part_in[pair] = pair_out[pair]
    for d in range(1, half):
        pair_copy(d, True).wait_recv()
    for g in range(groups):
        strips = []
        for j in range(ny):
            k = g * ny + j
            if k < OFFSETS:
                strip = part_in[:, :, k * 128 : (k + 1) * 128].astype(f32)
                strips.append(jnp.sum(strip, axis=0))
            else:
                strips.append(jnp.zeros((slice_y, 128), f32))
        turned = jnp.concatenate(strips, axis=0).T
        piece[:, g] = turned.reshape(nx, slice_x, channels).astype(bf16)

    def piece_copy(d, arriving):
        other = lax.rem(x + d, nx)
        place = other if arriving else x
        return pltpu.make_async_remote_copy(
            src_ref=piece.at[other],
            dst_ref=piece_in.at[place],
            send_sem=wx_send.at[other],
            recv_sem=wx_recv.at[place],
            device_id=(other, y),
            device_id_type=MESH,
        )

    for d in range(1, nx):
        piece_copy(d, False).start()

    scatter(1, 2, steps)
    send_back(1)

    piece_in[x] = piece[x]
    for d in range(1, nx):
        piece_copy(d, True).wait_recv()
    scale = 1.0 / jnp.sqrt(total)
    for g in range(groups):
        summed = jnp.sum(piece_in[:, g].astype(f32), axis=0) * scale
        for j in range(ny):
            if g * ny + j < OFFSETS:
                gw_out[g * ny + j] = summed[:, j * slice_y : (j + 1) * slice_y]

    for q in range(2):
        for s, (dx, dy) in enumerate(directions):
            @pl.when(exists(dx, dy))
            def _(q=q, s=s):
                back_copy(q, s, True).wait_recv()
    pick = jnp.concatenate([along_rows(send[s : s + 1, :], rows) for s in range(8)], axis=1)
    added = jnp.dot(
        pick, returned[...].reshape(8 * 2 * window, channels), preferred_element_type=f32
    )
    gf_out[...] = (own_tab[...] + added).astype(bf16)

    for s, (dx, dy) in enumerate(directions):
        @pl.when(exists(dx, dy))
        def _(s=s):
            halo_copy(s).wait_send()
            for q in range(2):
                back_copy(q, s, False).wait_send()
    mate_copy().wait_send()
    for d in range(1, half):
        pair_copy(d, False).wait_send()
    for d in range(1, nx):
        piece_copy(d, False).wait_send()


def per_device(features, live_count, neighbour_map, send_rows, weight, gain, shift, cotangent):
    nx, ny = lax.axis_size("bx"), lax.axis_size("by")
    rows, channels = features.shape[2:]
    halo = send_rows.shape[3]
    block, window = rows // 2, halo // 2
    slice_x, slice_y = channels // nx, channels // ny
    groups = -(-OFFSETS // ny)
    vmem = pl.BlockSpec(memory_space=pltpu.VMEM)
    hbm = pl.BlockSpec(memory_space=pltpu.HBM)
    dma = pltpu.SemaphoreType.DMA
    activated, grad_features, grad_weight = pl.pallas_call(
        functools.partial(kernel, nx, ny),
        out_shape=(
            jax.ShapeDtypeStruct((rows, channels), bf16),
            jax.ShapeDtypeStruct((rows, channels), bf16),
            jax.ShapeDtypeStruct((OFFSETS, slice_x, slice_y), f32),
        ),
        in_specs=[
            pl.BlockSpec(memory_space=pltpu.SMEM), hbm, hbm, hbm, hbm, vmem, vmem, hbm,
        ],
        out_specs=(vmem, vmem, vmem),
        scratch_shapes=[
            pltpu.VMEM((rows, channels), bf16),
            pltpu.VMEM((OFFSETS * rows // 128, 128), jnp.int32),
            pltpu.VMEM((8, halo), jnp.int32),
            pltpu.VMEM((OFFSETS * channels, channels), bf16),
            pltpu.VMEM((rows, channels), bf16),
            pltpu.VMEM((2, block, OFFSETS * block), bf16),
            pltpu.VMEM((2, 8, window, channels), bf16),
            pltpu.VMEM((2, 8, window, channels), bf16),
            pltpu.VMEM((32, rows), jnp.int32),
            pltpu.VMEM((rows, 128), jnp.int32),
            pltpu.VMEM((2, block, 2 * channels), bf16),
            pltpu.VMEM((rows, OFFSETS * channels), bf16),
            pltpu.VMEM((rows, channels), bf16),
            pltpu.VMEM((rows, channels), bf16),
            pltpu.VMEM((block, 2 * channels), f32),
            pltpu.VMEM((rows, channels), f32),
            pltpu.VMEM((2, 8, window, channels), bf16),
            pltpu.VMEM((8, halo, channels), bf16),
            pltpu.VMEM((2, ny, 8, channels), f32),
            pltpu.VMEM((2, nx, 8, channels), f32),
            pltpu.VMEM((2, ny // 2, slice_y, OFFSETS * channels), bf16),
            pltpu.VMEM((ny // 2, slice_y, OFFSETS * channels), bf16),
            pltpu.VMEM((ny // 2, slice_y, OFFSETS * channels), bf16),
            pltpu.VMEM((ny // 2, slice_y, OFFSETS * channels), bf16),
            pltpu.VMEM((nx, groups, slice_x, channels), bf16),
            pltpu.VMEM((nx, groups, slice_x, channels), bf16),
            dma((8,)), dma((8,)),
            dma((2, ny)), dma((2, ny)),
            dma((2, nx)), dma((2, nx)),
            dma((2, 8)), dma((2, 8)),
            dma((1,)), dma((1,)),
            dma((ny // 2,)), dma((ny // 2,)),
            dma((nx,)), dma((nx,)),
            dma((5,)),
        ],
        compiler_params=pltpu.CompilerParams(
            collective_id=0, has_side_effects=True, vmem_limit_bytes=52 * 1024 * 1024
        ),
    )(
        live_count,
        features[0, 0],
        neighbour_map.reshape(-1, 128),
        send_rows[0, 0],
        weight,
        gain.reshape(1, -1),
        shift.reshape(1, -1),
        cotangent[0, 0],
    )
    return activated[None, None], grad_features[None, None], grad_weight


def solution(mesh):
    return jax.shard_map(
        per_device,
        mesh=mesh,
        in_specs=(
            P("bx", "by", None, None),
            P("bx", "by"),
            P("bx", "by", None, None),
            P("bx", "by", None, None),
            P(),
            P(),
            P(),
            P("bx", "by", None, None),
        ),
        out_specs=(P("bx", "by", None, None), P("bx", "by", None, None), P(None, "bx", "by")),
        check_vma=False,
    )
```
